128 devices in a mesh: img: 8 (over z, core), txt: 16 (over y, x).
Axes of the slice: x: 4, y: 4, z: 4, core: 2. Of those that a mesh axis runs over, the one named last changes fastest.
Arguments:
- picture_features: float32 [14336, 1280], P(('img', 'txt'))
- caption_features: float32 [14336, 1280], P(('img', 'txt'))
- softness_factor: float32 [1], replicated, may hold values from 0.3 to 0.6
- picture_cost_sensitivity: float32 [14336], P('img'), may hold values from 0.2 to 5
- caption_cost_sensitivity: float32 [14336], P(('img', 'txt')), may hold values from 0.2 to 5
Outputs:
- image_to_text_loss: float32 [14336], P(('img', 'txt'))
- text_to_image_loss: float32 [14336], P(('img', 'txt'))
- image_grad: float32 [14336, 1280], P(('img', 'txt'))
- text_grad: float32 [14336, 1280], P(('img', 'txt'))
The draws below stay inside these ranges and needn't reach their ends.
All inputs are finite; a program needn't handle non-finite values.
Results may differ from the reference program's by a relative error of at most 0.0003.
Values sent between devices are 32-bit elements; how exact they have to be, the bound alone decides.
No kernel may reach another device: no remote copies, remote signals or barrier semaphores. Data moves between devices by JAX's collectives and lax.ppermute only.
A program may use at most 128 MiB of HBM per device.

```python
import math
import jax
import jax.numpy as jnp
from jax import lax

E = 1280
B = 14336


def shared_parts(key):
    spread = E ** (-0.25)
    base = jax.random.normal(jax.random.fold_in(key, 101), (B, E), jnp.float32) * spread
    return base


def draw_picture_features(key, part):
    base = shared_parts(key)
    return base


def draw_caption_features(key, part):
    base = shared_parts(key)
    key = jax.random.fold_in(key, 2)
    spread = E ** (-0.25)
    noise = jax.random.normal(key, (B, E), jnp.float32) * spread
    return 0.04 * base + noise


def shard_levels(stream_key, shape, pieces, least, high):
    factor_of, own = 1.0, jax.random.fold_in(stream_key, 6)
    for position, blocks in pieces:
        draws = jnp.exp(jax.random.uniform(jax.random.fold_in(own, position), (blocks,), jnp.float32, least / len(pieces), high / len(pieces)))
        factor_of = factor_of * jnp.repeat(draws, shape[position] // blocks).reshape([-1 if axis == position else 1 for axis in range(len(shape))])
    return factor_of


def setup_inputs(seed: int = 0) -> dict:
    seeds = jax.random.split(jax.random.key(seed), 6)
    return {
        "picture_features": draw_picture_features(jax.random.fold_in(seeds[5], 71), 0),
        "caption_features": draw_caption_features(jax.random.fold_in(seeds[5], 71), 0),
        "softness_factor": jnp.clip(jnp.exp(jax.random.uniform(seeds[2], (1,), jnp.float32, math.log(0.3), math.log(0.6))), 0.3, 0.6),
        "picture_cost_sensitivity": jnp.clip(jnp.exp(math.log(5.0) - 3.218876 * jax.random.uniform(seeds[3], (B,), jnp.float32) ** shard_levels(seeds[3], (B,), ((0, 8),), -0.2, 0.2)), 0.2, 5.0),
        "caption_cost_sensitivity": jnp.clip(jnp.exp(math.log(5.0) - 3.218876 * jax.random.uniform(seeds[4], (B,), jnp.float32) ** shard_levels(seeds[4], (B,), ((0, 128),), -0.2, 0.2)), 0.2, 5.0),
    }


def sharpened_scores(first_factor, second_factor, scaling_exponent):
    inner_products = lax.dot_general(first_factor, second_factor, (((1,), (1,)), ((), ())), precision=lax.Precision.HIGHEST, preferred_element_type=jnp.float32)
    return inner_products / scaling_exponent


def reference(picture_features, caption_features, softness_factor, picture_cost_sensitivity, caption_cost_sensitivity):
    scaling_exponent = softness_factor[0]
    total = picture_features.shape[0]
    block = math.gcd(total, 512)
    starts = jnp.arange(total // block, dtype=jnp.int32) * block
    positions = jnp.arange(total, dtype=jnp.int32)

    def logsumexp_partition(similarity_scores):
        peak = jnp.max(similarity_scores, axis=1)
        return peak + jnp.log(jnp.sum(jnp.exp(similarity_scores - peak[:, None]), axis=1))

    def row_stats(start):
        picture_quantity = lax.dynamic_slice_in_dim(picture_features, start, block, 0)
        return logsumexp_partition(sharpened_scores(picture_quantity, caption_features, scaling_exponent))

    def col_stats(start):
        picture_quantity = lax.dynamic_slice_in_dim(caption_features, start, block, 0)
        return logsumexp_partition(sharpened_scores(picture_quantity, picture_features, scaling_exponent))

    row_lse = lax.map(row_stats, starts).reshape(total)
    col_lse = lax.map(col_stats, starts).reshape(total)
    matched_pair_scores = jnp.sum(picture_features * caption_features, axis=1) / scaling_exponent
    image_to_text_loss = row_lse - matched_pair_scores
    text_to_image_loss = col_lse - matched_pair_scores

    def image_embedding_block(start):
        picture_quantity = lax.dynamic_slice_in_dim(picture_features, start, block, 0)
        similarity_scores = sharpened_scores(picture_quantity, caption_features, scaling_exponent)
        ident = start + jnp.arange(block, dtype=jnp.int32)
        unit = (ident[:, None] == positions[None, :]).astype(jnp.float32)
        weight = lax.dynamic_slice_in_dim(picture_cost_sensitivity, start, block, 0)
        lse_rows = lax.dynamic_slice_in_dim(row_lse, start, block, 0)
        backprop_fn = weight[:, None] * (jnp.exp(similarity_scores - lse_rows[:, None]) - unit) + caption_cost_sensitivity[None, :] * (jnp.exp(similarity_scores - col_lse[None, :]) - unit)
        return jnp.dot(backprop_fn, caption_features, precision=lax.Precision.HIGHEST, preferred_element_type=jnp.float32) / scaling_exponent

    def text_block(start):
        picture_quantity = lax.dynamic_slice_in_dim(caption_features, start, block, 0)
        similarity_scores = sharpened_scores(picture_quantity, picture_features, scaling_exponent)
        ident = start + jnp.arange(block, dtype=jnp.int32)
        unit = (ident[:, None] == positions[None, :]).astype(jnp.float32)
        weight = lax.dynamic_slice_in_dim(caption_cost_sensitivity, start, block, 0)
        lse_cols = lax.dynamic_slice_in_dim(col_lse, start, block, 0)
        backprop_fn = weight[:, None] * (jnp.exp(similarity_scores - lse_cols[:, None]) - unit) + picture_cost_sensitivity[None, :] * (jnp.exp(similarity_scores - row_lse[None, :]) - unit)
        return jnp.dot(backprop_fn, picture_features, precision=lax.Precision.HIGHEST, preferred_element_type=jnp.float32) / scaling_exponent

    image_grad = lax.map(image_embedding_block, starts).reshape(total, E)
    text_grad = lax.map(text_block, starts).reshape(total, E)
    return (image_to_text_loss, text_to_image_loss, image_grad, text_grad)
```

```python
import functools

import jax
import jax.numpy as jnp
from jax import lax
from jax.experimental import pallas as pl
from jax.experimental.pallas import tpu as pltpu
from jax.sharding import PartitionSpec as P

F32 = jnp.float32
OWN = 112
BLK = 2 * OWN
E = 1280
HALF = 4 * BLK
MIB = 1024 * 1024

HOPS = {
    "a": ((1, 0, 0), (3, 0, 0)),
    "b": ((0, 1, 0), (0, 3, 0)),
    "c": ((0, 0, 1), (0, 0, 3)),
    "abc": ((1, 1, 1), (3, 3, 3)),
}
BITS = (0, 1, 2, 4, 3, 6, 5, 7)
PLACE = tuple(BITS.index(v) for v in range(8))


def device(z, core, y, x):
    return (z * 2 + core) * 16 + y * 4 + x


def chips():
    return [(z, core, y, x) for z in range(4) for core in range(2) for y in range(4) for x in range(4)]


def move(block, name):
    pairs = []
    for z, core, y, x in chips():
        dx, dy, dz = HOPS[name][core]
        pairs.append((device(z, core, y, x), device(z ^ dz, core, y ^ dy, x ^ dx)))
    return lax.ppermute(block, ("img", "txt"), pairs)


def swap_cores(block):
    pairs = [(device(z, core, y, x), device(z, 1 - core, y, x)) for z, core, y, x in chips()]
    return lax.ppermute(block, ("img", "txt"), pairs)


def role_groups():
    groups = []
    for z, core, y, x in chips():
        step = 1 if core == 0 else 3
        group = [
            device(z ^ dz, core, y ^ dy, x ^ dx) for dz in (0, step) for dy in (0, step) for dx in (0, step)
        ]
        if group[0] == min(group):
            groups.append(group)
    return groups


def dot(first, second, dims):
    return lax.dot_general(
        first, second, (dims, ((), ())), precision=lax.Precision.HIGH, preferred_element_type=F32
    )


NT = ((1,), (1,))
NN = ((1,), (0,))


def params(flops, vmem):
    return dict(
        compiler_params=pltpu.CompilerParams(vmem_limit_bytes=vmem * MIB),
        cost_estimate=pl.CostEstimate(flops=flops, bytes_accessed=20_000_000, transcendentals=0),
    )


def sds(shape):
    return jax.ShapeDtypeStruct(shape, F32)


def whole(shape):
    return pl.BlockSpec(shape, lambda i: (0,) * len(shape))


def rows_at(width, first, count):
    return pl.BlockSpec((BLK, width), lambda i: (jnp.clip(i - first, 0, count - 1), 0))


ANY = pl.BlockSpec(memory_space=pl.ANY)
SMEM = pl.BlockSpec(memory_space=pltpu.SMEM)


def to_row(column):
    return jnp.transpose(jnp.broadcast_to(column, (BLK, 128)))[0:1, :]


def to_column(row):
    return jnp.transpose(jnp.broadcast_to(row, (128, BLK)))[:, 0:1]


def row_stats(stats):
    top = functools.reduce(jnp.maximum, [m for m, _ in stats])
    return top, sum(l * jnp.exp(m - top) for m, l in stats)


def put_stats(stats_ref, at, top, total, add):
    top, total = to_row(top), to_row(total)
    if add:
        old_top, old_total = stats_ref[at : at + 1, :], stats_ref[8 + at : 9 + at, :]
        new = jnp.maximum(old_top, top)
        total = old_total * jnp.exp(old_top - new) + total * jnp.exp(top - new)
        top = new
    stats_ref[at : at + 1, :] = top
    stats_ref[8 + at : 9 + at, :] = total


def logits_kernel(plan, a_blocks, b_blocks, shapes, add_stats, t_ref, *refs):
    n_a, n_b, n_s = len(a_blocks), len(b_blocks), len(shapes)
    stats_in, refs = (refs[:2], refs[2:]) if add_stats else (None, refs)
    a_hbm, b_hbm, refs = refs[:n_a], refs[n_a : n_a + n_b], refs[n_a + n_b :]
    s_hbm, stats_ref, refs = refs[:n_s], refs[n_s], refs[n_s + 1 :]
    a, b, s_refs, sems, out_sems = refs[0], refs[1], refs[2 : 2 + n_s], refs[-2], refs[-1]
    scale = 1.0 / t_ref[0]
    held = {}
    for k, (side, block) in enumerate([("a", v) for v in a_blocks] + [("b", v) for v in b_blocks]):
        hbm, dst, first = (a_hbm, a, a_blocks) if side == "a" else (b_hbm, b, b_blocks)
        at = first.index(block)
        held[side, block] = pltpu.make_async_copy(hbm[at], dst.at[pl.ds(at * BLK, BLK)], sems.at[k])
    needs = []
    for first, count, products in plan:
        for b_first, b_count, _ in products:
            needs += [("a", v) for v in range(first, first + count)]
            needs += [("b", v) for v in range(b_first, b_first + b_count)]
    for need in dict.fromkeys(needs):
        held[need].start()
    if add_stats:
        stats_ref[...] = stats_in[0][...]
        stats_ref[16:17, :] = stats_in[1][...]
    else:
        stats_ref[...] = jnp.zeros(stats_ref.shape, F32)
    stored = []
    for first, count, products in plan:
        stats = []
        for b_first, b_count, out in products:
            wanted = [("a", v) for v in range(first, first + count)] + [("b", v) for v in range(b_first, b_first + b_count)]
            for need in wanted:
                if need in held:
                    held.pop(need).wait()
            a_at, b_at = a_blocks.index(first) * BLK, b_blocks.index(b_first) * BLK
            s = dot(a[a_at : a_at + count * BLK, :], b[b_at : b_at + b_count * BLK, :], NT) * scale
            row = (first - shapes[out][0]) * BLK
            s_refs[out][row : row + count * BLK, :] = s
            at = pl.ds(row, count * BLK)
            copy = pltpu.make_async_copy(s_refs[out].at[at], s_hbm[out].at[at], out_sems.at[len(stored)])
            copy.start()
            stored.append(copy)
            top = jnp.max(s, axis=1, keepdims=True)
            stats.append((top, jnp.sum(jnp.exp(s - top), axis=1, keepdims=True)))
        top, total = row_stats(stats)
        for k in range(count):
            at = slice(k * BLK, (k + 1) * BLK)
            put_stats(stats_ref, first + k, top[at], total[at], add_stats and first < add_stats)
    for copy in stored:
        copy.wait()


def logits(name, cost, plan, a, b, shapes, t, add_stats=0, stats=()):
    vmem = pl.BlockSpec(memory_space=pltpu.VMEM)
    parts = sum(len(products) for _, _, products in plan)
    return pl.pallas_call(
        functools.partial(logits_kernel, plan, tuple(a), tuple(b), shapes, add_stats),
        in_specs=[SMEM] + [vmem] * len(stats) + [ANY] * (len(a) + len(b)),
        out_specs=[ANY] * len(shapes) + [vmem],
        out_shape=[sds(shape[1:]) for shape in shapes] + [sds((24, BLK))],
        scratch_shapes=[pltpu.VMEM((len(a) * BLK, E), F32), pltpu.VMEM((len(b) * BLK, E), F32)]
        + [pltpu.VMEM(shape[1:], F32) for shape in shapes]
        + [pltpu.SemaphoreType.DMA((len(a) + len(b),)), pltpu.SemaphoreType.DMA((parts,))],
        name=name,
        **params(cost, 12 + 7 * len(b) // 2),
    )(t, *stats, *a.values(), *b.values())


def combine_kernel(rank_ref, stats_ref, shift_ref):
    rank = rank_ref[0]
    for at, bits in enumerate(BITS):
        tops, totals = [], []
        for sender in range(8):
            place = place_of(jnp.bitwise_xor(jnp.bitwise_xor(rank, bits), sender))
            tops.append(stats_ref[sender, pl.ds(place, 1), :])
            totals.append(stats_ref[sender, pl.ds(8 + place, 1), :])
        top = functools.reduce(jnp.maximum, tops)
        total = sum(l * jnp.exp(m - top) for m, l in zip(tops, totals))
        weight = stats_ref[jnp.bitwise_xor(rank, bits), 16:17, :]
        shift_ref[at : at + 1, :] = top + jnp.log(total) - jnp.log(weight)


def place_of(bits):
    place = jnp.int32(0)
    for v in range(8):
        place = jnp.where(bits == v, PLACE[v], place)
    return place


def combine(rank, stats):
    return pl.pallas_call(
        combine_kernel,
        in_specs=[pl.BlockSpec(memory_space=pltpu.SMEM), pl.BlockSpec(memory_space=pltpu.VMEM)],
        out_shape=sds((8, BLK)),
        name="combine",
        **params(1_000_000, 2),
    )(rank, stats)


def grad_kernel(first, count, own, shift_a, shift_b, pair_ref, *refs):
    s_hbm, b_hbm, out_hbm, refs = refs[:2], refs[2:10], refs[10 : 10 + count], refs[10 + count :]
    s_all, b, out_refs, s_sems, b_sems, out_sems = refs
    row = (first % 4) * BLK
    s_copies = [
        [
            pltpu.make_async_copy(
                s_hbm[p].at[pl.ds(row + k * BLK, BLK)],
                s_all.at[pl.ds(k * BLK, BLK), pl.ds(p * HALF, HALF)],
                s_sems.at[2 * k + p],
            )
            for p in range(2)
        ]
        for k in range(count)
    ]
    b_copies = [pltpu.make_async_copy(b_hbm[v], b.at[pl.ds(v * BLK, BLK)], b_sems.at[v]) for v in range(8)]
    for p in range(2):
        s_copies[0][p].start()
        for v in range(4):
            b_copies[4 * p + v].start()
    for k in range(1, count):
        for p in range(2):
            s_copies[k][p].start()
    stored = []
    for k in range(count):
        rows = to_column(shift_a[first + k : first + k + 1, :])
        at = slice(k * BLK, (k + 1) * BLK)

        def sensitivity(columns):
            s = s_all[at, columns]
            return jnp.exp(s - rows) + jnp.exp(s - shift_b[:, columns])

        if k == 0:
            value = None
            for p in range(2):
                columns = slice(p * HALF, (p + 1) * HALF)
                s_copies[0][p].wait()
                g = sensitivity(columns)
                if own and p == 0:
                    same = lax.broadcasted_iota(jnp.int32, g.shape, 0) == lax.broadcasted_iota(jnp.int32, g.shape, 1)
                    g = g - jnp.where(same, jnp.broadcast_to(pair_ref[...], g.shape), 0.0)
                for v in range(4):
                    b_copies[4 * p + v].wait()
                term = dot(g, b[columns, :], NN)
                value = term if value is None else value + term
            for j in range(1, count):
                for p in range(2):
                    s_copies[j][p].wait()
        else:
            value = dot(sensitivity(slice(0, 2 * HALF)), b[...], NN)
        out_refs[at, :] = value
        copy = pltpu.make_async_copy(out_refs.at[pl.ds(k * BLK, BLK)], out_hbm[k], out_sems.at[k])
        copy.start()
        stored.append(copy)
    for copy in stored:
        copy.wait()


def grad(name, blocks, own, shift_a, shift_b, pair, s, b):
    count = len(blocks)
    vmem = pl.BlockSpec(memory_space=pltpu.VMEM)
    return pl.pallas_call(
        functools.partial(grad_kernel, blocks[0], count, own),
        in_specs=[vmem] * 3 + [ANY] * 10,
        out_specs=[ANY] * count,
        out_shape=[sds((BLK, E))] * count,
        scratch_shapes=[
            pltpu.VMEM((count * BLK, 2 * HALF), F32), pltpu.VMEM((8 * BLK, E), F32), pltpu.VMEM((count * BLK, E), F32),
            pltpu.SemaphoreType.DMA((2 * count,)), pltpu.SemaphoreType.DMA((8,)), pltpu.SemaphoreType.DMA((count,)),
        ],
        name=name,
        **params(8_000_000_000 * count, 32),
    )(shift_a, shift_b, pair, *s, *b)


def body(pictures, captions, softness_factor, picture_weights, caption_weights):
    core = lax.axis_index("img") % 2
    txt_at = lax.axis_index("txt")
    z, y, x = lax.axis_index("img") // 2, txt_at // 4, txt_at % 4
    is_image = core == 0

    def in_order(mine, other):
        return jnp.where(is_image, mine, other), jnp.where(is_image, other, mine)

    own_weights = lax.dynamic_slice_in_dim(picture_weights, txt_at * OWN, OWN, 0)
    weights = jnp.stack([own_weights, caption_weights])
    other_weights = swap_cores(weights)
    first_weights, second_weights = in_order(weights, other_weights)
    pair_weights = jnp.concatenate([first_weights, second_weights], axis=1)
    role_weight = jnp.where(is_image, pair_weights[0:1], pair_weights[1:2])
    pair = jnp.pad(pair_weights[0:1] + pair_weights[1:2], ((0, 0), (0, HALF - BLK)))

    other = swap_cores(jnp.where(is_image, captions, pictures))
    a_own = jnp.concatenate(in_order(jnp.where(is_image, pictures, captions), other), axis=0)
    t = softness_factor
    a = [a_own] + [move(a_own, k) for k in "abc"]
    b = [swap_cores(a_own)]
    a += [move(a[1], "b"), move(a[2], "c"), move(a[3], "a")]
    b += [swap_cores(v) for v in a[1:4]]
    corner = move(a[5], "a")
    b += [swap_cores(v) for v in a[4:7]]
    snn, stats = logits(
        "logits_near", 12_000_000_000, ((0, 2, ((0, 4, 0),)), (2, 2, ((0, 4, 0),))),
        dict(enumerate(a[:4])), dict(enumerate(b[:4])), ((0, HALF, HALF),), t,
    )
    corner, stats = lax.optimization_barrier((corner, stats))
    a.append(corner)
    b.append(swap_cores(corner))
    snf, sff, sfn, stats = logits(
        "logits_far", 30_000_000_000,
        ((0, 2, ((4, 4, 0),)), (2, 2, ((4, 4, 0),)), (4, 2, ((4, 4, 1), (0, 4, 2))), (6, 2, ((4, 4, 1), (0, 4, 2)))),
        dict(enumerate(a)), dict(enumerate(b)), ((0, HALF, HALF), (4, HALF, HALF), (4, HALF, HALF)), t, 4,
        (stats, role_weight),
    )

    shifted = jnp.where(is_image, 0, 1)
    bit = lambda v: lax.shift_right_logical(v, shifted) % 2
    rank = (bit(z) * 4 + bit(y) * 2 + bit(x)).astype(jnp.int32).reshape(1)
    everyone = lax.all_to_all(
        jnp.broadcast_to(stats[None], (8, 24, BLK)), ("img", "txt"), split_axis=0, concat_axis=0,
        tiled=True, axis_index_groups=role_groups(),
    )
    shift_a = combine(rank, everyone)
    shift_b = swap_cores(shift_a)
    b_shift = shift_b.reshape(1, 2 * HALF)

    def terms(name, blocks, own, s):
        return grad(name, blocks, own, shift_a, b_shift, pair, s, b)

    far = terms("grad_far", (4, 5, 6, 7), False, (sfn, sff))
    sent = [move(far[0], "b"), move(far[1], "c"), move(far[2], "a")]
    corner = move(far[3], "abc")
    near = terms("grad_near", (1, 2, 3), False, (snn, snf))
    back = [move(p + q, k) for p, q, k in zip(near, sent, "abc")]
    own = terms("grad_own", (0,), True, (snn, snf))[0]
    softness = softness_factor[0]
    role_grad = (own + corner + back[0] + back[1] + back[2]) / softness
    mine = jnp.where(is_image, role_grad[:OWN], role_grad[OWN:])
    theirs = swap_cores(jnp.where(is_image, role_grad[OWN:], role_grad[:OWN]))
    image_grad = jnp.where(is_image, mine, theirs)
    text_grad = jnp.where(is_image, theirs, mine)

    diag = jnp.sum(pictures * captions, axis=1) / softness
    pairs = lambda v: jnp.where(is_image, v[:OWN], v[OWN:])
    row_shift = jnp.where(is_image, shift_a[0], shift_b[0])
    col_shift = jnp.where(is_image, shift_b[0], shift_a[0])
    image_to_text_loss = pairs(row_shift) + jnp.log(own_weights) - diag
    text_to_image_loss = pairs(col_shift) + jnp.log(caption_weights) - diag
    return (image_to_text_loss, text_to_image_loss, image_grad, text_grad)


def solution(mesh):
    return jax.shard_map(
        body,
        mesh=mesh,
        in_specs=(
            P(("img", "txt"), None),
            P(("img", "txt"), None),
            P(),
            P("img"),
            P(("img", "txt")),
        ),
        out_specs=(
            P(("img", "txt")),
            P(("img", "txt")),
            P(("img", "txt"), None),
            P(("img", "txt"), None),
        ),
        check_vma=False,
    )
```

```python
import functools

import jax
import jax.numpy as jnp
from jax import lax
from jax.experimental import pallas as pl
from jax.experimental.pallas import tpu as pltpu
from jax.sharding import PartitionSpec as P

F32 = jnp.float32
OWN = 112
BLK = 2 * OWN
E = 1280
HALF = 4 * BLK
MIB = 1024 * 1024

HOPS = {
    "a": ((1, 0, 0), (3, 0, 0)),
    "b": ((0, 1, 0), (0, 3, 0)),
    "c": ((0, 0, 1), (0, 0, 3)),
    "abc": ((1, 1, 1), (3, 3, 3)),
}
BITS = (0, 1, 2, 4, 3, 6, 5, 7)
PLACE = tuple(BITS.index(v) for v in range(8))


def device(z, core, y, x):
    return (z * 2 + core) * 16 + y * 4 + x


def chips():
    return [(z, core, y, x) for z in range(4) for core in range(2) for y in range(4) for x in range(4)]


def move(block, name):
    pairs = []
    for z, core, y, x in chips():
        dx, dy, dz = HOPS[name][core]
        pairs.append((device(z, core, y, x), device(z ^ dz, core, y ^ dy, x ^ dx)))
    return lax.ppermute(block, ("img", "txt"), pairs)


def swap_cores(block):
    pairs = [(device(z, core, y, x), device(z, 1 - core, y, x)) for z, core, y, x in chips()]
    return lax.ppermute(block, ("img", "txt"), pairs)


def role_groups():
    groups = []
    for z, core, y, x in chips():
        step = 1 if core == 0 else 3
        group = [
            device(z ^ dz, core, y ^ dy, x ^ dx) for dz in (0, step) for dy in (0, step) for dx in (0, step)
        ]
        if group[0] == min(group):
            groups.append(group)
    return groups


def dot(first, second, dims):
    return lax.dot_general(
        first, second, (dims, ((), ())), precision=lax.Precision.HIGH, preferred_element_type=F32
    )


NT = ((1,), (1,))
NN = ((1,), (0,))


def params(flops, vmem):
    return dict(
        compiler_params=pltpu.CompilerParams(vmem_limit_bytes=vmem * MIB),
        cost_estimate=pl.CostEstimate(flops=flops, bytes_accessed=20_000_000, transcendentals=0),
    )


def sds(shape):
    return jax.ShapeDtypeStruct(shape, F32)


def whole(shape):
    return pl.BlockSpec(shape, lambda i: (0,) * len(shape))


def rows_at(width, first, count):
    return pl.BlockSpec((BLK, width), lambda i: (jnp.clip(i - first, 0, count - 1), 0))


ANY = pl.BlockSpec(memory_space=pl.ANY)
HBM = pl.BlockSpec(memory_space=pltpu.HBM)
SMEM = pl.BlockSpec(memory_space=pltpu.SMEM)


def in_hbm(v):
    return pltpu.with_memory_space_constraint(v, pltpu.HBM)


def to_row(column):
    return jnp.transpose(jnp.broadcast_to(column, (BLK, 128)))[0:1, :]


def to_column(row):
    return jnp.transpose(jnp.broadcast_to(row, (128, BLK)))[:, 0:1]


def row_stats(stats):
    top = functools.reduce(jnp.maximum, [m for m, _ in stats])
    return top, sum(l * jnp.exp(m - top) for m, l in stats)


def put_stats(stats_ref, at, top, total, add):
    top, total = to_row(top), to_row(total)
    if add:
        old_top, old_total = stats_ref[at : at + 1, :], stats_ref[8 + at : 9 + at, :]
        new = jnp.maximum(old_top, top)
        total = old_total * jnp.exp(old_top - new) + total * jnp.exp(top - new)
        top = new
    stats_ref[at : at + 1, :] = top
    stats_ref[8 + at : 9 + at, :] = total


def logits_kernel(plan, a_blocks, b_blocks, n_s, add_stats, t_ref, *refs):
    n_a, n_b = len(a_blocks), len(b_blocks)
    stats_in, refs = (refs[:2], refs[3:]) if add_stats else (None, refs)
    a_hbm, b_hbm, refs = refs[:n_a], refs[n_a : n_a + n_b], refs[n_a + n_b :]
    s_hbm, stats_ref, refs = refs[:n_s], refs[n_s], refs[n_s + 1 :]
    if add_stats:
        b_out, refs = refs[0], refs[1:]
    a, b, s_buf, sems, out_sems = refs
    scale = 1.0 / t_ref[0]
    held = {}
    for k, (side, block) in enumerate([("a", v) for v in a_blocks] + [("b", v) for v in b_blocks]):
        hbm, dst, first = (a_hbm, a, a_blocks) if side == "a" else (b_hbm, b, b_blocks)
        at = first.index(block)
        held[side, block] = pltpu.make_async_copy(hbm[at], dst.at[pl.ds(at * BLK, BLK)], sems.at[k])
    needs = []
    for first, count, halves in plan:
        for b_first in halves:
            needs += [("a", v) for v in range(first, first + count)] + [("b", v) for v in range(b_first, b_first + 4)]
    for need in dict.fromkeys(needs):
        held[need].start()
    if add_stats:
        stats_ref[...] = stats_in[0][...]
        stats_ref[16:17, :] = stats_in[1][...]
    else:
        stats_ref[...] = jnp.zeros(stats_ref.shape, F32)
    stored, done = [], 0
    for first, count, halves in plan:
        stats = []
        for b_first in halves:
            for need in [("a", v) for v in range(first, first + count)] + [("b", v) for v in range(b_first, b_first + 4)]:
                if need in held:
                    held.pop(need).wait()
            if add_stats and not held and b_out is not None:
                copy = pltpu.make_async_copy(b, b_out, out_sems.at[out_sems.shape[0] - 1])
                copy.start()
                stored.append(copy)
                b_out = None
            a_at, b_at = a_blocks.index(first) * BLK, b_blocks.index(b_first) * BLK
            s = dot(a[a_at : a_at + count * BLK, :], b[b_at : b_at + HALF, :], NT) * scale
            slot = pl.ds(done * 2 * BLK, count * BLK)
            s_buf[slot, :] = s
            copy = pltpu.make_async_copy(
                s_buf.at[slot],
                s_hbm[first // 4].at[pl.ds(first % 4 * BLK, count * BLK), pl.ds(b_first * BLK, HALF)],
                out_sems.at[done],
            )
            copy.start()
            stored.append(copy)
            done += 1
            top = jnp.max(s, axis=1, keepdims=True)
            stats.append((top, jnp.sum(jnp.exp(s - top), axis=1, keepdims=True)))
        top, total = row_stats(stats)
        for k in range(count):
            at = slice(k * BLK, (k + 1) * BLK)
            put_stats(stats_ref, first + k, top[at], total[at], add_stats and first < add_stats)
    for copy in stored:
        copy.wait()


def logits(name, cost, plan, a, b, t, add_stats=0, near=()):
    vmem = pl.BlockSpec(memory_space=pltpu.VMEM)
    parts = sum(len(halves) for _, _, halves in plan)
    n_s = 2 if near else 1
    return pl.pallas_call(
        functools.partial(logits_kernel, plan, tuple(a), tuple(b), n_s, add_stats),
        in_specs=[SMEM] + ([vmem, vmem, HBM] if near else []) + [HBM] * (len(a) + len(b)),
        out_specs=[HBM] * n_s + [vmem] + ([HBM] if near else []),
        out_shape=[pltpu.HBM((HALF, 2 * HALF), F32)] * n_s
        + [sds((24, BLK))]
        + ([pltpu.HBM((8 * BLK, E), F32)] if near else []),
        input_output_aliases={3: 0} if near else {},
        scratch_shapes=[
            pltpu.VMEM((len(a) * BLK, E), F32), pltpu.VMEM((len(b) * BLK, E), F32), pltpu.VMEM((parts * 2 * BLK, HALF), F32),
            pltpu.SemaphoreType.DMA((len(a) + len(b),)), pltpu.SemaphoreType.DMA((parts + (1 if near else 0),)),
        ],
        name=name,
        **params(cost, 12 + 7 * len(b) // 2),
    )(t, *near[:2], *[in_hbm(v) for v in (*near[2:], *a.values(), *b.values())])


def combine_kernel(rank_ref, stats_ref, shift_ref):
    rank = rank_ref[0]
    for at, bits in enumerate(BITS):
        tops, totals = [], []
        for sender in range(8):
            place = place_of(jnp.bitwise_xor(jnp.bitwise_xor(rank, bits), sender))
            tops.append(stats_ref[sender, pl.ds(place, 1), :])
            totals.append(stats_ref[sender, pl.ds(8 + place, 1), :])
        top = functools.reduce(jnp.maximum, tops)
        total = sum(l * jnp.exp(m - top) for m, l in zip(tops, totals))
        weight = stats_ref[jnp.bitwise_xor(rank, bits), 16:17, :]
        shift_ref[at : at + 1, :] = top + jnp.log(total) - jnp.log(weight)


def place_of(bits):
    place = jnp.int32(0)
    for v in range(8):
        place = jnp.where(bits == v, PLACE[v], place)
    return place


def combine(rank, stats):
    return pl.pallas_call(
        combine_kernel,
        in_specs=[pl.BlockSpec(memory_space=pltpu.SMEM), pl.BlockSpec(memory_space=pltpu.VMEM)],
        out_shape=sds((8, BLK)),
        name="combine",
        **params(1_000_000, 2),
    )(rank, stats)


def sensitivity(s, rows, cols):
    return jnp.exp(s - rows) + jnp.exp(s - cols)


def grad_kernel(first, count, own, shift_a, shift_b, pair_ref, s_ref, b, *refs):
    out_hbm, (out_refs, out_sems) = refs[:count], refs[count:]
    stored = []
    for k in range(count):
        rows = to_column(shift_a[first + k : first + k + 1, :])
        at = slice(k * BLK, (k + 1) * BLK)
        row = ((first + k) % 4) * BLK
        g = sensitivity(s_ref[row : row + BLK, :], rows, shift_b[...])
        if own and k == 0:
            same = lax.broadcasted_iota(jnp.int32, g.shape, 0) == lax.broadcasted_iota(jnp.int32, g.shape, 1)
            g = g - jnp.where(same, jnp.broadcast_to(pair_ref[...], g.shape), 0.0)
        out_refs[at, :] = dot(g, b[...], NN)
        copy = pltpu.make_async_copy(out_refs.at[pl.ds(k * BLK, BLK)], out_hbm[k], out_sems.at[k])
        copy.start()
        stored.append(copy)
    for copy in stored:
        copy.wait()


def grad(name, blocks, own, shift_a, shift_b, pair, s, b):
    count = len(blocks)
    vmem = pl.BlockSpec(memory_space=pltpu.VMEM)
    return pl.pallas_call(
        functools.partial(grad_kernel, blocks[0], count, own),
        in_specs=[vmem] * 5,
        out_specs=[ANY] * count,
        out_shape=[sds((BLK, E))] * count,
        scratch_shapes=[pltpu.VMEM((count * BLK, E), F32), pltpu.SemaphoreType.DMA((count,))],
        name=name,
        **params(6_000_000_000 * count, 16),
    )(shift_a, shift_b, pair, *[pltpu.with_memory_space_constraint(v, pltpu.VMEM) for v in (s, b)])


def body(pictures, captions, softness_factor, picture_weights, caption_weights):
    core = lax.axis_index("img") % 2
    txt_at = lax.axis_index("txt")
    z, y, x = lax.axis_index("img") // 2, txt_at // 4, txt_at % 4
    is_image = core == 0

    def in_order(mine, other):
        return jnp.where(is_image, mine, other), jnp.where(is_image, other, mine)

    own_weights = lax.dynamic_slice_in_dim(picture_weights, txt_at * OWN, OWN, 0)
    weights = jnp.stack([own_weights, caption_weights])
    other_weights = swap_cores(weights)
    first_weights, second_weights = in_order(weights, other_weights)
    pair_weights = jnp.concatenate([first_weights, second_weights], axis=1)
    role_weight = jnp.where(is_image, pair_weights[0:1], pair_weights[1:2])
    pair = jnp.pad(pair_weights[0:1] + pair_weights[1:2], ((0, 0), (0, 2 * HALF - BLK)))

    other = swap_cores(jnp.where(is_image, captions, pictures))
    a_own = jnp.concatenate(in_order(jnp.where(is_image, pictures, captions), other), axis=0)
    t = softness_factor
    a = [a_own] + [move(a_own, k) for k in "abc"]
    b = [swap_cores(a_own)]
    a += [move(a[1], "b"), move(a[2], "c"), move(a[3], "a")]
    b += [swap_cores(v) for v in a[1:4]]
    corner = move(a[5], "a")
    b += [swap_cores(v) for v in a[4:7]]
    s_near, stats = logits(
        "logits_near", 12_000_000_000, ((0, 2, (0,)), (2, 2, (0,))), dict(enumerate(a[:4])), dict(enumerate(b[:4])), t
    )
    corner, stats = lax.optimization_barrier((corner, stats))
    a.append(corner)
    b.append(swap_cores(corner))
    s_near, s_far, stats, b_all = logits(
        "logits_far", 30_000_000_000, ((0, 2, (4,)), (2, 2, (4,)), (4, 2, (4, 0)), (6, 2, (4, 0))),
        dict(enumerate(a)), dict(enumerate(b)), t, 4, (stats, role_weight, s_near),
    )

    shifted = jnp.where(is_image, 0, 1)
    bit = lambda v: lax.shift_right_logical(v, shifted) % 2
    rank = (bit(z) * 4 + bit(y) * 2 + bit(x)).astype(jnp.int32).reshape(1)
    everyone = lax.all_to_all(
        jnp.broadcast_to(stats[None], (8, 24, BLK)), ("img", "txt"), split_axis=0, concat_axis=0,
        tiled=True, axis_index_groups=role_groups(),
    )
    shift_a = combine(rank, everyone)
    shift_b = swap_cores(shift_a)
    b_shift = shift_b.reshape(1, 2 * HALF)

    def terms(name, blocks, own, s):
        return grad(name, blocks, own, shift_a, b_shift, pair, s, b_all)

    corner = move(terms("grad_abc", (7,), False, s_far)[0], "abc")
    far = terms("grad_far", (4, 5, 6), False, s_far)
    *far, corner = lax.optimization_barrier((*far, corner))
    sent = [move(far[0], "b"), move(far[1], "c"), move(far[2], "a")]
    near = terms("grad_near", (1, 2, 3), False, s_near)
    back = [move(p + q, k) for p, q, k in zip(near, sent, "abc")]
    own = terms("grad_own", (0,), True, s_near)[0]
    softness = softness_factor[0]
    role_grad = (own + corner + back[0] + back[1] + back[2]) / softness
    mine = jnp.where(is_image, role_grad[:OWN], role_grad[OWN:])
    theirs = swap_cores(jnp.where(is_image, role_grad[OWN:], role_grad[:OWN]))
    image_grad = jnp.where(is_image, mine, theirs)
    text_grad = jnp.where(is_image, theirs, mine)

    diag = jnp.sum(pictures * captions, axis=1) / softness
    pairs = lambda v: jnp.where(is_image, v[:OWN], v[OWN:])
    row_shift = jnp.where(is_image, shift_a[0], shift_b[0])
    col_shift = jnp.where(is_image, shift_b[0], shift_a[0])
    image_to_text_loss = pairs(row_shift) + jnp.log(own_weights) - diag
    text_to_image_loss = pairs(col_shift) + jnp.log(caption_weights) - diag
    return (image_to_text_loss, text_to_image_loss, image_grad, text_grad)


def solution(mesh):
    return jax.shard_map(
        body,
        mesh=mesh,
        in_specs=(
            P(("img", "txt"), None),
            P(("img", "txt"), None),
            P(),
            P("img"),
            P(("img", "txt")),
        ),
        out_specs=(
            P(("img", "txt")),
            P(("img", "txt")),
            P(("img", "txt"), None),
            P(("img", "txt"), None),
        ),
        check_vma=False,
    )
```

```python
import functools

import jax
import jax.numpy as jnp
from jax import lax
from jax.experimental import pallas as pl
from jax.experimental.pallas import tpu as pltpu
from jax.sharding import PartitionSpec as P

F32 = jnp.float32
OWN = 112
BLK = 2 * OWN
E = 1280
HALF = 4 * BLK
MIB = 1024 * 1024

HOPS = {
    "a": ((1, 0, 0), (3, 0, 0)),
    "b": ((0, 1, 0), (0, 3, 0)),
    "c": ((0, 0, 1), (0, 0, 3)),
    "abc": ((1, 1, 1), (3, 3, 3)),
}
BITS = (0, 1, 2, 4, 3, 6, 5, 7)
PLACE = tuple(BITS.index(v) for v in range(8))


def device(z, core, y, x):
    return (z * 2 + core) * 16 + y * 4 + x


def chips():
    return [(z, core, y, x) for z in range(4) for core in range(2) for y in range(4) for x in range(4)]


def move(block, name):
    pairs = []
    for z, core, y, x in chips():
        dx, dy, dz = HOPS[name][core]
        pairs.append((device(z, core, y, x), device(z ^ dz, core, y ^ dy, x ^ dx)))
    return lax.ppermute(block, ("img", "txt"), pairs)


def swap_cores(block):
    pairs = [(device(z, core, y, x), device(z, 1 - core, y, x)) for z, core, y, x in chips()]
    return lax.ppermute(block, ("img", "txt"), pairs)


def role_groups():
    groups = []
    for z, core, y, x in chips():
        step = 1 if core == 0 else 3
        group = [
            device(z ^ dz, core, y ^ dy, x ^ dx) for dz in (0, step) for dy in (0, step) for dx in (0, step)
        ]
        if group[0] == min(group):
            groups.append(group)
    return groups


def dot(first, second, dims):
    return lax.dot_general(
        first, second, (dims, ((), ())), precision=lax.Precision.HIGH, preferred_element_type=F32
    )


NT = ((1,), (1,))
NN = ((1,), (0,))


def params(flops, vmem):
    return dict(
        compiler_params=pltpu.CompilerParams(vmem_limit_bytes=vmem * MIB),
        cost_estimate=pl.CostEstimate(flops=flops, bytes_accessed=20_000_000, transcendentals=0),
    )


def sds(shape):
    return jax.ShapeDtypeStruct(shape, F32)


def whole(shape):
    return pl.BlockSpec(shape, lambda i: (0,) * len(shape))


def rows_at(width, first, count):
    return pl.BlockSpec((BLK, width), lambda i: (jnp.clip(i - first, 0, count - 1), 0))


ANY = pl.BlockSpec(memory_space=pl.ANY)
HBM = pl.BlockSpec(memory_space=pltpu.HBM)
SMEM = pl.BlockSpec(memory_space=pltpu.SMEM)


def in_hbm(v):
    return pltpu.with_memory_space_constraint(v, pltpu.HBM)


def to_row(column):
    return jnp.transpose(jnp.broadcast_to(column, (BLK, 128)))[0:1, :]


def to_column(row):
    return jnp.transpose(jnp.broadcast_to(row, (128, BLK)))[:, 0:1]


def row_stats(stats):
    top = functools.reduce(jnp.maximum, [m for m, _ in stats])
    return top, sum(l * jnp.exp(m - top) for m, l in stats)


def put_stats(stats_ref, at, top, total, add):
    top, total = to_row(top), to_row(total)
    if add:
        old_top, old_total = stats_ref[at : at + 1, :], stats_ref[8 + at : 9 + at, :]
        new = jnp.maximum(old_top, top)
        total = old_total * jnp.exp(old_top - new) + total * jnp.exp(top - new)
        top = new
    stats_ref[at : at + 1, :] = top
    stats_ref[8 + at : 9 + at, :] = total


def logits_kernel(plan, a_blocks, b_blocks, n_s, add_stats, t_ref, *refs):
    n_a, n_b = len(a_blocks), len(b_blocks)
    stats_in, refs = refs[0], refs[2:] if add_stats else refs[1:]
    a_hbm, b_hbm, refs = refs[:n_a], refs[n_a : n_a + n_b], refs[n_a + n_b :]
    s_hbm, stats_ref, refs = refs[:n_s], refs[n_s], refs[n_s + 1 :]
    if add_stats:
        b_out, refs = refs[0], refs[1:]
    a, b, s_buf, sems, out_sems = refs
    scale = 1.0 / t_ref[0]
    held = {}
    for k, (side, block) in enumerate([("a", v) for v in a_blocks] + [("b", v) for v in b_blocks]):
        hbm, dst, first = (a_hbm, a, a_blocks) if side == "a" else (b_hbm, b, b_blocks)
        at = first.index(block)
        held[side, block] = pltpu.make_async_copy(hbm[at], dst.at[pl.ds(at * BLK, BLK)], sems.at[k])
    needs = []
    for first, count, halves in plan:
        for b_first in halves:
            needs += [("a", v) for v in range(first, first + count)] + [("b", v) for v in range(b_first, b_first + 4)]
    for need in dict.fromkeys(needs):
        held[need].start()
    if add_stats:
        stats_ref[...] = stats_in[...]
    else:
        stats_ref[...] = jnp.zeros(stats_ref.shape, F32)
        stats_ref[16:17, :] = stats_in[...]
    stored, done = [], 0
    for first, count, halves in plan:
        stats = []
        for b_first in halves:
            for need in [("a", v) for v in range(first, first + count)] + [("b", v) for v in range(b_first, b_first + 4)]:
                if need in held:
                    held.pop(need).wait()
            if add_stats and not held and b_out is not None:
                copy = pltpu.make_async_copy(b, b_out, out_sems.at[out_sems.shape[0] - 1])
                copy.start()
                stored.append(copy)
                b_out = None
            a_at, b_at = a_blocks.index(first) * BLK, b_blocks.index(b_first) * BLK
            s = dot(a[a_at : a_at + count * BLK, :], b[b_at : b_at + HALF, :], NT) * scale
            slot = pl.ds(done * 2 * BLK, count * BLK)
            s_buf[slot, :] = s
            copy = pltpu.make_async_copy(
                s_buf.at[slot],
                s_hbm[first // 4].at[pl.ds(first % 4 * BLK, count * BLK), pl.ds(b_first * BLK, HALF)],
                out_sems.at[done],
            )
            copy.start()
            stored.append(copy)
            done += 1
            top = jnp.max(s, axis=1, keepdims=True)
            stats.append((top, jnp.sum(jnp.exp(s - top), axis=1, keepdims=True)))
        top, total = row_stats(stats)
        for k in range(count):
            at = slice(k * BLK, (k + 1) * BLK)
            put_stats(stats_ref, first + k, top[at], total[at], add_stats and first < add_stats)
    for copy in stored:
        copy.wait()


def logits(name, cost, vmem_limit, plan, a, b, t, stats, add_stats=0, near=()):
    vmem = pl.BlockSpec(memory_space=pltpu.VMEM)
    parts = sum(len(halves) for _, _, halves in plan)
    n_s = 2 if near else 1
    return pl.pallas_call(
        functools.partial(logits_kernel, plan, tuple(a), tuple(b), n_s, add_stats),
        in_specs=[SMEM, vmem] + [HBM] * len(near) + [ANY] * (len(a) + len(b)),
        out_specs=[HBM] * n_s + [vmem] + ([HBM] if near else []),
        out_shape=[pltpu.HBM((HALF, 2 * HALF), F32)] * n_s
        + [sds((24, BLK))]
        + ([pltpu.HBM((8 * BLK, E), F32)] if near else []),
        input_output_aliases={2: 0} if near else {},
        scratch_shapes=[
            pltpu.VMEM((len(a) * BLK, E), F32), pltpu.VMEM((len(b) * BLK, E), F32), pltpu.VMEM((parts * 2 * BLK, HALF), F32),
            pltpu.SemaphoreType.DMA((len(a) + len(b),)), pltpu.SemaphoreType.DMA((parts + (1 if near else 0),)),
        ],
        name=name,
        **params(cost, vmem_limit),
    )(t, stats, *[in_hbm(v) for v in near], *a.values(), *b.values())


def combine_kernel(rank_ref, stats_ref, shift_ref):
    rank = rank_ref[0]
    for at, bits in enumerate(BITS):
        tops, totals = [], []
        for sender in range(8):
            place = place_of(jnp.bitwise_xor(jnp.bitwise_xor(rank, bits), sender))
            tops.append(stats_ref[sender, pl.ds(place, 1), :])
            totals.append(stats_ref[sender, pl.ds(8 + place, 1), :])
        top = functools.reduce(jnp.maximum, tops)
        total = sum(l * jnp.exp(m - top) for m, l in zip(tops, totals))
        weight = stats_ref[jnp.bitwise_xor(rank, bits), 16:17, :]
        shift_ref[at : at + 1, :] = top + jnp.log(total) - jnp.log(weight)


def place_of(bits):
    place = jnp.int32(0)
    for v in range(8):
        place = jnp.where(bits == v, PLACE[v], place)
    return place


def combine(rank, stats):
    return pl.pallas_call(
        combine_kernel,
        in_specs=[pl.BlockSpec(memory_space=pltpu.SMEM), pl.BlockSpec(memory_space=pltpu.VMEM)],
        out_shape=sds((8, BLK)),
        name="combine",
        **params(1_000_000, 2),
    )(rank, stats)


def sensitivity(s, rows, cols):
    return jnp.exp(s - rows) + jnp.exp(s - cols)


def grad_kernel(first, count, own, shift_a, shift_b, pair_ref, s_ref, b, *refs):
    out_hbm, (out_refs, out_sems) = refs[:count], refs[count:]
    stored = []
    for k in range(count):
        rows = to_column(shift_a[first + k : first + k + 1, :])
        at = slice(k * BLK, (k + 1) * BLK)
        row = ((first + k) % 4) * BLK
        g = sensitivity(s_ref[row : row + BLK, :], rows, shift_b[...])
        if own and k == 0:
            same = lax.broadcasted_iota(jnp.int32, g.shape, 0) == lax.broadcasted_iota(jnp.int32, g.shape, 1)
            g = g - jnp.where(same, jnp.broadcast_to(pair_ref[...], g.shape), 0.0)
        out_refs[at, :] = dot(g, b[...], NN)
        copy = pltpu.make_async_copy(out_refs.at[pl.ds(k * BLK, BLK)], out_hbm[k], out_sems.at[k])
        copy.start()
        stored.append(copy)
    for copy in stored:
        copy.wait()


def grad(name, blocks, own, shift_a, shift_b, pair, s, b):
    count = len(blocks)
    vmem = pl.BlockSpec(memory_space=pltpu.VMEM)
    return pl.pallas_call(
        functools.partial(grad_kernel, blocks[0], count, own),
        in_specs=[vmem] * 5,
        out_specs=[ANY] * count,
        out_shape=[sds((BLK, E))] * count,
        scratch_shapes=[pltpu.VMEM((count * BLK, E), F32), pltpu.SemaphoreType.DMA((count,))],
        name=name,
        **params(6_000_000_000 * count, 16),
    )(shift_a, shift_b, pair, *[pltpu.with_memory_space_constraint(v, pltpu.VMEM) for v in (s, b)])


def body(pictures, captions, softness_factor, picture_weights, caption_weights):
    core = lax.axis_index("img") % 2
    txt_at = lax.axis_index("txt")
    z, y, x = lax.axis_index("img") // 2, txt_at // 4, txt_at % 4
    is_image = core == 0

    def in_order(mine, other):
        return jnp.where(is_image, mine, other), jnp.where(is_image, other, mine)

    own_weights = lax.dynamic_slice_in_dim(picture_weights, txt_at * OWN, OWN, 0)
    weights = jnp.stack([own_weights, caption_weights])
    other_weights = swap_cores(weights)
    first_weights, second_weights = in_order(weights, other_weights)
    pair_weights = jnp.concatenate([first_weights, second_weights], axis=1)
    role_weight = jnp.where(is_image, pair_weights[0:1], pair_weights[1:2])
    pair = jnp.pad(pair_weights[0:1] + pair_weights[1:2], ((0, 0), (0, 2 * HALF - BLK)))

    other = swap_cores(jnp.where(is_image, captions, pictures))
    a_own = jnp.concatenate(in_order(jnp.where(is_image, pictures, captions), other), axis=0)
    t = softness_factor
    a = [a_own] + [move(a_own, k) for k in "abc"]
    b = [swap_cores(a_own)]
    a += [move(a[1], "b"), move(a[2], "c"), move(a[3], "a")]
    b += [swap_cores(v) for v in a[1:4]]
    corner = move(a[5], "a")
    b += [swap_cores(v) for v in a[4:7]]
    s_near, stats = logits(
        "logits_near", 12_000_000_000, 18, ((0, 2, (0,)), (2, 2, (0,))), dict(enumerate(a[:4])), dict(enumerate(b[:4])),
        t, role_weight,
    )
    corner, stats = lax.optimization_barrier((corner, stats))
    a.append(corner)
    b.append(swap_cores(corner))
    s_near, s_far, stats, b_all = logits(
        "logits_far", 30_000_000_000, 34, ((0, 2, (4,)), (2, 2, (4,)), (4, 2, (4, 0)), (6, 2, (4, 0))),
        dict(enumerate(a)), dict(enumerate(b)), t, stats, 4, (s_near,),
    )

    shifted = jnp.where(is_image, 0, 1)
    bit = lambda v: lax.shift_right_logical(v, shifted) % 2
    rank = (bit(z) * 4 + bit(y) * 2 + bit(x)).astype(jnp.int32).reshape(1)
    everyone = lax.all_to_all(
        jnp.broadcast_to(stats[None], (8, 24, BLK)), ("img", "txt"), split_axis=0, concat_axis=0,
        tiled=True, axis_index_groups=role_groups(),
    )
    shift_a = combine(rank, everyone)
    shift_b = swap_cores(shift_a)
    b_shift = shift_b.reshape(1, 2 * HALF)

    def terms(name, blocks, own, s):
        return grad(name, blocks, own, shift_a, b_shift, pair, s, b_all)

    corner = move(terms("grad_abc", (7,), False, s_far)[0], "abc")
    far = terms("grad_far", (4, 5, 6), False, s_far)
    last, corner = lax.optimization_barrier((far[2], corner))
    sent = [move(far[0], "b"), move(far[1], "c"), move(last, "a")]
    near = terms("grad_near", (1, 2, 3), False, s_near)
    back = [move(p + q, k) for p, q, k in zip(near, sent, "abc")]
    own = terms("grad_own", (0,), True, s_near)[0]
    softness = softness_factor[0]
    role_grad = (own + corner + back[0] + back[1] + back[2]) / softness
    mine = jnp.where(is_image, role_grad[:OWN], role_grad[OWN:])
    theirs = swap_cores(jnp.where(is_image, role_grad[OWN:], role_grad[:OWN]))
    image_grad = jnp.where(is_image, mine, theirs)
    text_grad = jnp.where(is_image, theirs, mine)

    diag = jnp.sum(pictures * captions, axis=1) / softness
    pairs = lambda v: jnp.where(is_image, v[:OWN], v[OWN:])
    row_shift = jnp.where(is_image, shift_a[0], shift_b[0])
    col_shift = jnp.where(is_image, shift_b[0], shift_a[0])
    image_to_text_loss = pairs(row_shift) + jnp.log(own_weights) - diag
    text_to_image_loss = pairs(col_shift) + jnp.log(caption_weights) - diag
    return (image_to_text_loss, text_to_image_loss, image_grad, text_grad)


def solution(mesh):
    return jax.shard_map(
        body,
        mesh=mesh,
        in_specs=(
            P(("img", "txt"), None),
            P(("img", "txt"), None),
            P(),
            P("img"),
            P(("img", "txt")),
        ),
        out_specs=(
            P(("img", "txt")),
            P(("img", "txt")),
            P(("img", "txt"), None),
            P(("img", "txt"), None),
        ),
        check_vma=False,
    )
```

```python
import functools

import jax
import jax.numpy as jnp
from jax import lax
from jax.experimental import pallas as pl
from jax.experimental.pallas import tpu as pltpu
from jax.sharding import PartitionSpec as P

F32 = jnp.float32
OWN = 112
BLK = 2 * OWN
E = 1280
HALF = 4 * BLK
MIB = 1024 * 1024

HOPS = {
    "a": ((1, 0, 0), (3, 0, 0)),
    "b": ((0, 1, 0), (0, 3, 0)),
    "c": ((0, 0, 1), (0, 0, 3)),
    "abc": ((1, 1, 1), (3, 3, 3)),
}
BITS = (0, 1, 2, 4, 3, 6, 5, 7)
PLACE = tuple(BITS.index(v) for v in range(8))


def device(z, core, y, x):
    return (z * 2 + core) * 16 + y * 4 + x


def chips():
    return [(z, core, y, x) for z in range(4) for core in range(2) for y in range(4) for x in range(4)]


def move(block, name):
    pairs = []
    for z, core, y, x in chips():
        dx, dy, dz = HOPS[name][core]
        pairs.append((device(z, core, y, x), device(z ^ dz, core, y ^ dy, x ^ dx)))
    return lax.ppermute(block, ("img", "txt"), pairs)


def swap_cores(block):
    pairs = [(device(z, core, y, x), device(z, 1 - core, y, x)) for z, core, y, x in chips()]
    return lax.ppermute(block, ("img", "txt"), pairs)


def role_groups():
    groups = []
    for z, core, y, x in chips():
        step = 1 if core == 0 else 3
        group = [
            device(z ^ dz, core, y ^ dy, x ^ dx) for dz in (0, step) for dy in (0, step) for dx in (0, step)
        ]
        if group[0] == min(group):
            groups.append(group)
    return groups


def dot(first, second, dims):
    return lax.dot_general(
        first, second, (dims, ((), ())), precision=lax.Precision.HIGH, preferred_element_type=F32
    )


NT = ((1,), (1,))
NN = ((1,), (0,))


def params(flops, vmem):
    return dict(
        compiler_params=pltpu.CompilerParams(vmem_limit_bytes=vmem * MIB),
        cost_estimate=pl.CostEstimate(flops=flops, bytes_accessed=20_000_000, transcendentals=0),
    )


def sds(shape):
    return jax.ShapeDtypeStruct(shape, F32)


def whole(shape):
    return pl.BlockSpec(shape, lambda i: (0,) * len(shape))


def rows_at(width, first, count):
    return pl.BlockSpec((BLK, width), lambda i: (jnp.clip(i - first, 0, count - 1), 0))


ANY = pl.BlockSpec(memory_space=pl.ANY)
HBM = pl.BlockSpec(memory_space=pltpu.HBM)
SMEM = pl.BlockSpec(memory_space=pltpu.SMEM)


def in_hbm(v):
    return pltpu.with_memory_space_constraint(v, pltpu.HBM)


def to_row(column):
    return jnp.transpose(jnp.broadcast_to(column, (BLK, 128)))[0:1, :]


def to_column(row):
    return jnp.transpose(jnp.broadcast_to(row, (128, BLK)))[:, 0:1]


def row_stats(stats):
    top = functools.reduce(jnp.maximum, [m for m, _ in stats])
    return top, sum(l * jnp.exp(m - top) for m, l in stats)


def put_stats(stats_ref, at, top, total, add):
    top, total = to_row(top), to_row(total)
    if add:
        old_top, old_total = stats_ref[at : at + 1, :], stats_ref[8 + at : 9 + at, :]
        new = jnp.maximum(old_top, top)
        total = old_total * jnp.exp(old_top - new) + total * jnp.exp(top - new)
        top = new
    stats_ref[at : at + 1, :] = top
    stats_ref[8 + at : 9 + at, :] = total


def logits_kernel(plan, a_blocks, b_blocks, n_s, add_stats, t_ref, *refs):
    n_a, n_b = len(a_blocks), len(b_blocks)
    stats_in, refs = (refs[:2], refs[3:]) if add_stats else (None, refs)
    a_hbm, b_hbm, refs = refs[:n_a], refs[n_a : n_a + n_b], refs[n_a + n_b :]
    s_hbm, stats_ref, refs = refs[:n_s], refs[n_s], refs[n_s + 1 :]
    if add_stats:
        b_out, refs = refs[0], refs[1:]
    a, b, s_buf, sems, out_sems = refs
    scale = 1.0 / t_ref[0]
    held = {}
    for k, (side, block) in enumerate([("a", v) for v in a_blocks] + [("b", v) for v in b_blocks]):
        hbm, dst, first = (a_hbm, a, a_blocks) if side == "a" else (b_hbm, b, b_blocks)
        at = first.index(block)
        held[side, block] = pltpu.make_async_copy(hbm[at], dst.at[pl.ds(at * BLK, BLK)], sems.at[k])
    needs = []
    for first, count, halves in plan:
        for b_first in halves:
            needs += [("a", v) for v in range(first, first + count)] + [("b", v) for v in range(b_first, b_first + 4)]
    for need in dict.fromkeys(needs):
        held[need].start()
    if add_stats:
        stats_ref[...] = stats_in[0][...]
        stats_ref[16:17, :] = stats_in[1][...]
    else:
        stats_ref[...] = jnp.zeros(stats_ref.shape, F32)
    stored, done = [], 0
    for first, count, halves in plan:
        stats = []
        for b_first in halves:
            for need in [("a", v) for v in range(first, first + count)] + [("b", v) for v in range(b_first, b_first + 4)]:
                if need in held:
                    held.pop(need).wait()
            if add_stats and not held and b_out is not None:
                copy = pltpu.make_async_copy(b, b_out, out_sems.at[out_sems.shape[0] - 1])
                copy.start()
                stored.append(copy)
                b_out = None
            a_at, b_at = a_blocks.index(first) * BLK, b_blocks.index(b_first) * BLK
            s = dot(a[a_at : a_at + count * BLK, :], b[b_at : b_at + HALF, :], NT) * scale
            slot = pl.ds(done * 2 * BLK, count * BLK)
            s_buf[slot, :] = s
            copy = pltpu.make_async_copy(
                s_buf.at[slot],
                s_hbm[first // 4].at[pl.ds(first % 4 * BLK, count * BLK), pl.ds(b_first * BLK, HALF)],
                out_sems.at[done],
            )
            copy.start()
            stored.append(copy)
            done += 1
            top = jnp.max(s, axis=1, keepdims=True)
            stats.append((top, jnp.sum(jnp.exp(s - top), axis=1, keepdims=True)))
        top, total = row_stats(stats)
        for k in range(count):
            at = slice(k * BLK, (k + 1) * BLK)
            put_stats(stats_ref, first + k, top[at], total[at], add_stats and first < add_stats)
    for copy in stored:
        copy.wait()


def logits(name, cost, vmem_limit, plan, a, b, t, add_stats=0, near=()):
    vmem = pl.BlockSpec(memory_space=pltpu.VMEM)
    parts = sum(len(halves) for _, _, halves in plan)
    n_s = 2 if near else 1
    return pl.pallas_call(
        functools.partial(logits_kernel, plan, tuple(a), tuple(b), n_s, add_stats),
        in_specs=[SMEM] + ([vmem, vmem, HBM] if near else []) + [ANY] * (len(a) + len(b)),
        out_specs=[HBM] * n_s + [vmem] + ([HBM] if near else []),
        out_shape=[pltpu.HBM((HALF, 2 * HALF), F32)] * n_s
        + [sds((24, BLK))]
        + ([pltpu.HBM((8 * BLK, E), F32)] if near else []),
        input_output_aliases={3: 0} if near else {},
        scratch_shapes=[
            pltpu.VMEM((len(a) * BLK, E), F32), pltpu.VMEM((len(b) * BLK, E), F32), pltpu.VMEM((parts * 2 * BLK, HALF), F32),
            pltpu.SemaphoreType.DMA((len(a) + len(b),)), pltpu.SemaphoreType.DMA((parts + (1 if near else 0),)),
        ],
        name=name,
        **params(cost, vmem_limit),
    )(t, *near[:2], *[in_hbm(v) for v in near[2:]], *a.values(), *b.values())


def combine_kernel(rank_ref, stats_ref, shift_ref):
    rank = rank_ref[0]
    for at, bits in enumerate(BITS):
        tops, totals = [], []
        for sender in range(8):
            place = place_of(jnp.bitwise_xor(jnp.bitwise_xor(rank, bits), sender))
            tops.append(stats_ref[sender, pl.ds(place, 1), :])
            totals.append(stats_ref[sender, pl.ds(8 + place, 1), :])
        top = functools.reduce(jnp.maximum, tops)
        total = sum(l * jnp.exp(m - top) for m, l in zip(tops, totals))
        weight = stats_ref[jnp.bitwise_xor(rank, bits), 16:17, :]
        shift_ref[at : at + 1, :] = top + jnp.log(total) - jnp.log(weight)


def place_of(bits):
    place = jnp.int32(0)
    for v in range(8):
        place = jnp.where(bits == v, PLACE[v], place)
    return place


def combine(rank, stats):
    return pl.pallas_call(
        combine_kernel,
        in_specs=[pl.BlockSpec(memory_space=pltpu.SMEM), pl.BlockSpec(memory_space=pltpu.VMEM)],
        out_shape=sds((8, BLK)),
        name="combine",
        **params(1_000_000, 2),
    )(rank, stats)


def sensitivity(s, rows, cols):
    return jnp.exp(s - rows) + jnp.exp(s - cols)


def grad_kernel(first, count, own, shift_a, shift_b, pair_ref, s_ref, b, *refs):
    out_hbm, (out_refs, out_sems) = refs[:count], refs[count:]
    stored = []
    for k in range(count):
        rows = to_column(shift_a[first + k : first + k + 1, :])
        at = slice(k * BLK, (k + 1) * BLK)
        row = ((first + k) % 4) * BLK
        g = sensitivity(s_ref[row : row + BLK, :], rows, shift_b[...])
        if own and k == 0:
            same = lax.broadcasted_iota(jnp.int32, g.shape, 0) == lax.broadcasted_iota(jnp.int32, g.shape, 1)
            g = g - jnp.where(same, jnp.broadcast_to(pair_ref[...], g.shape), 0.0)
        out_refs[at, :] = dot(g, b[...], NN)
        copy = pltpu.make_async_copy(out_refs.at[pl.ds(k * BLK, BLK)], out_hbm[k], out_sems.at[k])
        copy.start()
        stored.append(copy)
    for copy in stored:
        copy.wait()


def grad(name, blocks, own, shift_a, shift_b, pair, s, b):
    count = len(blocks)
    vmem = pl.BlockSpec(memory_space=pltpu.VMEM)
    return pl.pallas_call(
        functools.partial(grad_kernel, blocks[0], count, own),
        in_specs=[vmem] * 5,
        out_specs=[ANY] * count,
        out_shape=[sds((BLK, E))] * count,
        scratch_shapes=[pltpu.VMEM((count * BLK, E), F32), pltpu.SemaphoreType.DMA((count,))],
        name=name,
        **params(6_000_000_000 * count, 16),
    )(shift_a, shift_b, pair, *[pltpu.with_memory_space_constraint(v, pltpu.VMEM) for v in (s, b)])


def body(pictures, captions, softness_factor, picture_weights, caption_weights):
    core = lax.axis_index("img") % 2
    txt_at = lax.axis_index("txt")
    z, y, x = lax.axis_index("img") // 2, txt_at // 4, txt_at % 4
    is_image = core == 0

    def in_order(mine, other):
        return jnp.where(is_image, mine, other), jnp.where(is_image, other, mine)

    own_weights = lax.dynamic_slice_in_dim(picture_weights, txt_at * OWN, OWN, 0)
    weights = jnp.stack([own_weights, caption_weights])
    other_weights = swap_cores(weights)
    first_weights, second_weights = in_order(weights, other_weights)
    pair_weights = jnp.concatenate([first_weights, second_weights], axis=1)
    role_weight = jnp.where(is_image, pair_weights[0:1], pair_weights[1:2])
    pair = jnp.pad(pair_weights[0:1] + pair_weights[1:2], ((0, 0), (0, 2 * HALF - BLK)))

    other = swap_cores(jnp.where(is_image, captions, pictures))
    a_own = jnp.concatenate(in_order(jnp.where(is_image, pictures, captions), other), axis=0)
    t = softness_factor
    a = [a_own] + [move(a_own, k) for k in "abc"]
    b = [swap_cores(a_own)]
    a += [move(a[1], "b"), move(a[2], "c"), move(a[3], "a")]
    b += [swap_cores(v) for v in a[1:4]]
    corner = move(a[5], "a")
    b += [swap_cores(v) for v in a[4:7]]
    s_near, stats = logits(
        "logits_near", 12_000_000_000, 18, ((0, 2, (0,)), (2, 2, (0,))), dict(enumerate(a[:4])), dict(enumerate(b[:4])),
        t,
    )
    corner, stats = lax.optimization_barrier((corner, stats))
    a.append(corner)
    b.append(swap_cores(corner))
    s_near, s_far, stats, b_all = logits(
        "logits_far", 30_000_000_000, 34, ((0, 2, (4,)), (2, 2, (4,)), (4, 2, (4, 0)), (6, 2, (4, 0))),
        dict(enumerate(a)), dict(enumerate(b)), t, 4, (stats, role_weight, s_near),
    )

    shifted = jnp.where(is_image, 0, 1)
    bit = lambda v: lax.shift_right_logical(v, shifted) % 2
    rank = (bit(z) * 4 + bit(y) * 2 + bit(x)).astype(jnp.int32).reshape(1)
    everyone = lax.all_to_all(
        jnp.broadcast_to(stats[None], (8, 24, BLK)), ("img", "txt"), split_axis=0, concat_axis=0,
        tiled=True, axis_index_groups=role_groups(),
    )
    shift_a = combine(rank, everyone)
    shift_b = swap_cores(shift_a)
    b_shift = shift_b.reshape(1, 2 * HALF)

    def terms(name, blocks, own, s):
        return grad(name, blocks, own, shift_a, b_shift, pair, s, b_all)

    corner = move(terms("grad_abc", (7,), False, s_far)[0], "abc")
    far = terms("grad_far", (4, 5, 6), False, s_far)
    last, corner = lax.optimization_barrier((far[2], corner))
    sent = [move(far[0], "b"), move(far[1], "c"), move(last, "a")]
    near = terms("grad_near", (1, 2, 3), False, s_near)
    back = [move(p + q, k) for p, q, k in zip(near, sent, "abc")]
    own = terms("grad_own", (0,), True, s_near)[0]
    softness = softness_factor[0]
    role_grad = (own + corner + back[0] + back[1] + back[2]) / softness
    mine = jnp.where(is_image, role_grad[:OWN], role_grad[OWN:])
    theirs = swap_cores(jnp.where(is_image, role_grad[OWN:], role_grad[:OWN]))
    image_grad = jnp.where(is_image, mine, theirs)
    text_grad = jnp.where(is_image, theirs, mine)

    diag = jnp.sum(pictures * captions, axis=1) / softness
    pairs = lambda v: jnp.where(is_image, v[:OWN], v[OWN:])
    row_shift = jnp.where(is_image, shift_a[0], shift_b[0])
    col_shift = jnp.where(is_image, shift_b[0], shift_a[0])
    image_to_text_loss = pairs(row_shift) + jnp.log(own_weights) - diag
    text_to_image_loss = pairs(col_shift) + jnp.log(caption_weights) - diag
    return (image_to_text_loss, text_to_image_loss, image_grad, text_grad)


def solution(mesh):
    return jax.shard_map(
        body,
        mesh=mesh,
        in_specs=(
            P(("img", "txt"), None),
            P(("img", "txt"), None),
            P(),
            P("img"),
            P(("img", "txt")),
        ),
        out_specs=(
            P(("img", "txt")),
            P(("img", "txt")),
            P(("img", "txt"), None),
            P(("img", "txt"), None),
        ),
        check_vma=False,
    )
```

```python
import functools

import jax
import jax.numpy as jnp
from jax import lax
from jax.experimental import pallas as pl
from jax.experimental.pallas import tpu as pltpu
from jax.sharding import PartitionSpec as P

F32 = jnp.float32
OWN = 112
BLK = 2 * OWN
E = 1280
HALF = 4 * BLK
MIB = 1024 * 1024

HOPS = {
    "a": ((1, 0, 0), (3, 0, 0)),
    "b": ((0, 1, 0), (0, 3, 0)),
    "c": ((0, 0, 1), (0, 0, 3)),
    "abc": ((1, 1, 1), (3, 3, 3)),
}
BITS = (0, 1, 2, 4, 3, 6, 5, 7)
PLACE = tuple(BITS.index(v) for v in range(8))


def device(z, core, y, x):
    return (z * 2 + core) * 16 + y * 4 + x


def chips():
    return [(z, core, y, x) for z in range(4) for core in range(2) for y in range(4) for x in range(4)]


def move(block, name):
    pairs = []
    for z, core, y, x in chips():
        dx, dy, dz = HOPS[name][core]
        pairs.append((device(z, core, y, x), device(z ^ dz, core, y ^ dy, x ^ dx)))
    return lax.ppermute(block, ("img", "txt"), pairs)


def swap_cores(block):
    pairs = [(device(z, core, y, x), device(z, 1 - core, y, x)) for z, core, y, x in chips()]
    return lax.ppermute(block, ("img", "txt"), pairs)


def role_groups():
    groups = []
    for z, core, y, x in chips():
        step = 1 if core == 0 else 3
        group = [
            device(z ^ dz, core, y ^ dy, x ^ dx) for dz in (0, step) for dy in (0, step) for dx in (0, step)
        ]
        if group[0] == min(group):
            groups.append(group)
    return groups


def dot(first, second, dims):
    return lax.dot_general(
        first, second, (dims, ((), ())), precision=lax.Precision.HIGH, preferred_element_type=F32
    )


NT = ((1,), (1,))
NN = ((1,), (0,))


def params(flops, vmem):
    return dict(
        compiler_params=pltpu.CompilerParams(vmem_limit_bytes=vmem * MIB),
        cost_estimate=pl.CostEstimate(flops=flops, bytes_accessed=20_000_000, transcendentals=0),
    )


def sds(shape):
    return jax.ShapeDtypeStruct(shape, F32)


def whole(shape):
    return pl.BlockSpec(shape, lambda i: (0,) * len(shape))


def rows_at(width, first, count):
    return pl.BlockSpec((BLK, width), lambda i: (jnp.clip(i - first, 0, count - 1), 0))


ANY = pl.BlockSpec(memory_space=pl.ANY)
HBM = pl.BlockSpec(memory_space=pltpu.HBM)
SMEM = pl.BlockSpec(memory_space=pltpu.SMEM)


def in_hbm(v):
    return pltpu.with_memory_space_constraint(v, pltpu.HBM)


def to_row(column):
    return jnp.transpose(jnp.broadcast_to(column, (BLK, 128)))[0:1, :]


def to_column(row):
    return jnp.transpose(jnp.broadcast_to(row, (128, BLK)))[:, 0:1]


def row_stats(stats):
    top = functools.reduce(jnp.maximum, [m for m, _ in stats])
    return top, sum(l * jnp.exp(m - top) for m, l in stats)


def put_stats(stats_ref, at, top, total, add):
    top, total = to_row(top), to_row(total)
    if add:
        old_top, old_total = stats_ref[at : at + 1, :], stats_ref[8 + at : 9 + at, :]
        new = jnp.maximum(old_top, top)
        total = old_total * jnp.exp(old_top - new) + total * jnp.exp(top - new)
        top = new
    stats_ref[at : at + 1, :] = top
    stats_ref[8 + at : 9 + at, :] = total


def logits_kernel(plan, a_blocks, b_blocks, n_s, add_stats, t_ref, *refs):
    n_a, n_b = len(a_blocks), len(b_blocks)
    stats_in, refs = refs[0], refs[2:] if add_stats else refs[1:]
    a_hbm, b_hbm, refs = refs[:n_a], refs[n_a : n_a + n_b], refs[n_a + n_b :]
    s_hbm, stats_ref, refs = refs[:n_s], refs[n_s], refs[n_s + 1 :]
    if add_stats:
        b_out, refs = refs[0], refs[1:]
    a, b, s_buf, sems, out_sems = refs
    scale = 1.0 / t_ref[0]
    held = {}
    for k, (side, block) in enumerate([("a", v) for v in a_blocks] + [("b", v) for v in b_blocks]):
        hbm, dst, first = (a_hbm, a, a_blocks) if side == "a" else (b_hbm, b, b_blocks)
        at = first.index(block)
        held[side, block] = pltpu.make_async_copy(hbm[at], dst.at[pl.ds(at * BLK, BLK)], sems.at[k])
    needs = []
    for first, count, halves in plan:
        for b_first in halves:
            needs += [("a", v) for v in range(first, first + count)] + [("b", v) for v in range(b_first, b_first + 4)]
    for need in dict.fromkeys(needs):
        held[need].start()
    if add_stats:
        stats_ref[...] = stats_in[...]
    else:
        stats_ref[...] = jnp.zeros(stats_ref.shape, F32)
        stats_ref[16:17, :] = stats_in[...]
    stored, done = [], 0
    for first, count, halves in plan:
        stats = []
        for b_first in halves:
            for need in [("a", v) for v in range(first, first + count)] + [("b", v) for v in range(b_first, b_first + 4)]:
                if need in held:
                    held.pop(need).wait()
            if add_stats and not held and b_out is not None:
                copy = pltpu.make_async_copy(b, b_out, out_sems.at[out_sems.shape[0] - 1])
                copy.start()
                stored.append(copy)
                b_out = None
            a_at, b_at = a_blocks.index(first) * BLK, b_blocks.index(b_first) * BLK
            s = dot(a[a_at : a_at + count * BLK, :], b[b_at : b_at + HALF, :], NT) * scale
            slot = pl.ds(done * 2 * BLK, count * BLK)
            s_buf[slot, :] = s
            copy = pltpu.make_async_copy(
                s_buf.at[slot],
                s_hbm[first // 4].at[pl.ds(first % 4 * BLK, count * BLK), pl.ds(b_first * BLK, HALF)],
                out_sems.at[done],
            )
            copy.start()
            stored.append(copy)
            done += 1
            top = jnp.max(s, axis=1, keepdims=True)
            stats.append((top, jnp.sum(jnp.exp(s - top), axis=1, keepdims=True)))
        top, total = row_stats(stats)
        for k in range(count):
            at = slice(k * BLK, (k + 1) * BLK)
            put_stats(stats_ref, first + k, top[at], total[at], add_stats and first < add_stats)
    for copy in stored:
        copy.wait()


def logits(name, cost, vmem_limit, plan, a, b, t, stats, add_stats=0, near=()):
    vmem = pl.BlockSpec(memory_space=pltpu.VMEM)
    parts = sum(len(halves) for _, _, halves in plan)
    n_s = 2 if near else 1
    return pl.pallas_call(
        functools.partial(logits_kernel, plan, tuple(a), tuple(b), n_s, add_stats),
        in_specs=[SMEM, vmem] + [HBM] * len(near) + [ANY] * (len(a) + len(b)),
        out_specs=[HBM] * n_s + [vmem] + ([HBM] if near else []),
        out_shape=[pltpu.HBM((HALF, 2 * HALF), F32)] * n_s
        + [sds((24, BLK))]
        + ([pltpu.HBM((8 * BLK, E), F32)] if near else []),
        input_output_aliases={2: 0} if near else {},
        scratch_shapes=[
            pltpu.VMEM((len(a) * BLK, E), F32), pltpu.VMEM((len(b) * BLK, E), F32), pltpu.VMEM((parts * 2 * BLK, HALF), F32),
            pltpu.SemaphoreType.DMA((len(a) + len(b),)), pltpu.SemaphoreType.DMA((parts + (1 if near else 0),)),
        ],
        name=name,
        **params(cost, vmem_limit),
    )(t, stats, *[in_hbm(v) for v in near], *a.values(), *b.values())


def combine_kernel(rank_ref, stats_ref, shift_ref):
    rank = rank_ref[0]
    for at, bits in enumerate(BITS):
        tops, totals = [], []
        for sender in range(8):
            place = place_of(jnp.bitwise_xor(jnp.bitwise_xor(rank, bits), sender))
            tops.append(stats_ref[sender, pl.ds(place, 1), :])
            totals.append(stats_ref[sender, pl.ds(8 + place, 1), :])
        top = functools.reduce(jnp.maximum, tops)
        total = sum(l * jnp.exp(m - top) for m, l in zip(tops, totals))
        weight = stats_ref[jnp.bitwise_xor(rank, bits), 16:17, :]
        shift_ref[at : at + 1, :] = top + jnp.log(total) - jnp.log(weight)


def place_of(bits):
    place = jnp.int32(0)
    for v in range(8):
        place = jnp.where(bits == v, PLACE[v], place)
    return place


def combine(rank, stats):
    return pl.pallas_call(
        combine_kernel,
        in_specs=[pl.BlockSpec(memory_space=pltpu.SMEM), pl.BlockSpec(memory_space=pltpu.VMEM)],
        out_shape=sds((8, BLK)),
        name="combine",
        **params(1_000_000, 2),
    )(rank, stats)


def sensitivity(s, rows, cols):
    return jnp.exp(s - rows) + jnp.exp(s - cols)


def grad_kernel(first, count, own, shift_a, shift_b, pair_ref, s_ref, b, *refs):
    out_hbm, (out_refs, out_sems) = refs[:count], refs[count:]
    stored = []
    for k in range(count):
        rows = to_column(shift_a[first + k : first + k + 1, :])
        at = slice(k * BLK, (k + 1) * BLK)
        row = ((first + k) % 4) * BLK
        g = sensitivity(s_ref[row : row + BLK, :], rows, shift_b[...])
        if own and k == 0:
            same = lax.broadcasted_iota(jnp.int32, g.shape, 0) == lax.broadcasted_iota(jnp.int32, g.shape, 1)
            g = g - jnp.where(same, jnp.broadcast_to(pair_ref[...], g.shape), 0.0)
        out_refs[at, :] = dot(g, b[...], NN)
        copy = pltpu.make_async_copy(out_refs.at[pl.ds(k * BLK, BLK)], out_hbm[k], out_sems.at[k])
        copy.start()
        stored.append(copy)
    for copy in stored:
        copy.wait()


def grad(name, blocks, own, shift_a, shift_b, pair, s, b):
    count = len(blocks)
    vmem = pl.BlockSpec(memory_space=pltpu.VMEM)
    return pl.pallas_call(
        functools.partial(grad_kernel, blocks[0], count, own),
        in_specs=[vmem] * 5,
        out_specs=[ANY] * count,
        out_shape=[sds((BLK, E))] * count,
        scratch_shapes=[pltpu.VMEM((count * BLK, E), F32), pltpu.SemaphoreType.DMA((count,))],
        name=name,
        **params(6_000_000_000 * count, 16),
    )(shift_a, shift_b, pair, *[pltpu.with_memory_space_constraint(v, pltpu.VMEM) for v in (s, b)])


def body(pictures, captions, softness_factor, picture_weights, caption_weights):
    core = lax.axis_index("img") % 2
    txt_at = lax.axis_index("txt")
    z, y, x = lax.axis_index("img") // 2, txt_at // 4, txt_at % 4
    is_image = core == 0

    def in_order(mine, other):
        return jnp.where(is_image, mine, other), jnp.where(is_image, other, mine)

    own_weights = lax.dynamic_slice_in_dim(picture_weights, txt_at * OWN, OWN, 0)
    weights = jnp.stack([own_weights, caption_weights])
    other = swap_cores(jnp.where(is_image, captions, pictures))
    other_weights = swap_cores(weights)
    other, other_weights = lax.optimization_barrier((other, other_weights))
    first_weights, second_weights = in_order(weights, other_weights)
    pair_weights = jnp.concatenate([first_weights, second_weights], axis=1)
    role_weight = jnp.where(is_image, pair_weights[0:1], pair_weights[1:2])
    pair = jnp.pad(pair_weights[0:1] + pair_weights[1:2], ((0, 0), (0, 2 * HALF - BLK)))

    a_own = jnp.concatenate(in_order(jnp.where(is_image, pictures, captions), other), axis=0)
    t = softness_factor
    a = [a_own] + [move(a_own, k) for k in "abc"]
    b = [swap_cores(a_own)]
    a += [move(a[1], "b"), move(a[2], "c"), move(a[3], "a")]
    b += [swap_cores(v) for v in a[1:4]]
    corner = move(a[5], "a")
    b += [swap_cores(v) for v in a[4:7]]
    s_near, stats = logits(
        "logits_near", 12_000_000_000, 18, ((0, 2, (0,)), (2, 2, (0,))), dict(enumerate(a[:4])), dict(enumerate(b[:4])),
        t, role_weight,
    )
    corner, stats = lax.optimization_barrier((corner, stats))
    a.append(corner)
    b.append(swap_cores(corner))
    s_near, s_far, stats, b_all = logits(
        "logits_far", 30_000_000_000, 34, ((0, 2, (4,)), (2, 2, (4,)), (4, 2, (4, 0)), (6, 2, (4, 0))),
        dict(enumerate(a)), dict(enumerate(b)), t, stats, 4, (s_near,),
    )

    shifted = jnp.where(is_image, 0, 1)
    bit = lambda v: lax.shift_right_logical(v, shifted) % 2
    rank = (bit(z) * 4 + bit(y) * 2 + bit(x)).astype(jnp.int32).reshape(1)
    everyone = lax.all_to_all(
        jnp.broadcast_to(stats[None], (8, 24, BLK)), ("img", "txt"), split_axis=0, concat_axis=0,
        tiled=True, axis_index_groups=role_groups(),
    )
    shift_a = combine(rank, everyone)
    shift_b = swap_cores(shift_a)
    b_shift = shift_b.reshape(1, 2 * HALF)

    def terms(name, blocks, own, s):
        return grad(name, blocks, own, shift_a, b_shift, pair, s, b_all)

    corner = move(terms("grad_abc", (7,), False, s_far)[0], "abc")
    far = terms("grad_far", (4, 5, 6), False, s_far)
    last, corner = lax.optimization_barrier((far[2], corner))
    sent = [move(far[0], "b"), move(far[1], "c"), move(last, "a")]
    near = terms("grad_near", (1, 2, 3), False, s_near)
    back = [move(p + q, k) for p, q, k in zip(near, sent, "abc")]
    own = terms("grad_own", (0,), True, s_near)[0]
    softness = softness_factor[0]
    role_grad = (own + corner + back[0] + back[1] + back[2]) / softness
    mine = jnp.where(is_image, role_grad[:OWN], role_grad[OWN:])
    theirs = swap_cores(jnp.where(is_image, role_grad[OWN:], role_grad[:OWN]))
    image_grad = jnp.where(is_image, mine, theirs)
    text_grad = jnp.where(is_image, theirs, mine)

    diag = jnp.sum(pictures * captions, axis=1) / softness
    pairs = lambda v: jnp.where(is_image, v[:OWN], v[OWN:])
    row_shift = jnp.where(is_image, shift_a[0], shift_b[0])
    col_shift = jnp.where(is_image, shift_b[0], shift_a[0])
    image_to_text_loss = pairs(row_shift) + jnp.log(own_weights) - diag
    text_to_image_loss = pairs(col_shift) + jnp.log(caption_weights) - diag
    return (image_to_text_loss, text_to_image_loss, image_grad, text_grad)


def solution(mesh):
    return jax.shard_map(
        body,
        mesh=mesh,
        in_specs=(
            P(("img", "txt"), None),
            P(("img", "txt"), None),
            P(),
            P("img"),
            P(("img", "txt")),
        ),
        out_specs=(
            P(("img", "txt")),
            P(("img", "txt")),
            P(("img", "txt"), None),
            P(("img", "txt"), None),
        ),
        check_vma=False,
    )
```
